32 devices in a mesh: sub: 8 (over y, x, core), rep: 4 (over z).
Axes of the slice: x: 2, y: 2, z: 4, core: 2. Of those that a mesh axis runs over, the one named last changes fastest.
Arguments:
- rhs: float32 [2048, 128], P('sub'), may hold values from -31 to 31
- schur_diag: bfloat16 [2048, 256], P('sub'), may hold values from -0.375 to 0.375
- precond: bfloat16 [2048, 512], P('sub'), may hold values from -0.25 to 0.25
- halo_ids: int32 [8, 2], P('sub'), may hold values from 0 to 15, as said below
- factors: bfloat16 [64, 1024, 1024], P(('sub', 'rep')), may hold values from -0.1875 to 0.1875
- couplings: bfloat16 [64, 1024, 512], P(('sub', 'rep')), may hold values from -0.09375 to 0.09375
- block_ids: int32 [64, 4], P(('sub', 'rep')), may hold values from 0 to 15
- counts: int32 [32], P(('sub', 'rep')), may hold values from 1 to 2, 40 in all
Outputs:
- solution: float32 [2048, 128], P('sub')
The draws below stay inside these ranges and needn't reach their ends.
Inputs may be any that keep to these rules, and one draw needn't show every extreme that they name: `halo_ids`: in row d the first 1 entries name blocks owned by index d - 1 of sub and the others blocks owned by index d + 1, cyclically; block b is owned by index b // 2. counts[i] belongs to device i of sub+rep, sub slowest; slots k with k % 2 >= counts[k // 2] are not part of the operator.
All inputs are finite; a program needn't handle non-finite values.
Results may differ from the reference program's by a relative error of at most 0.0031.
Values may be sent and summed in bfloat16 or wider, within the bound.
A program may use at most 64 MiB of HBM per device.

```python
import math
import jax
import jax.numpy as jnp
import numpy as np
from jax import lax

BLK = 1024
BI = 128
IFB = 4
HB = 2
NRHS = 128
NB_DEV = 2
GB_DEV = 2
GBLK = 16
G = 2048
EXT = 512
SLOTS = 64
N_SUB = 8
DEVICES = 32


def draw_rhs(key, part):
    key_scale, key_base = jax.random.split(jax.random.fold_in(key, 11), 2)
    scales = jnp.exp(jax.random.uniform(key_scale, (G, 1), minval=0.0, maxval=math.log(10.0)))
    rising = 1.0 + 2.0 * jnp.arange(G, dtype=jnp.float32)[:, None] / G
    base = jnp.clip(jax.random.normal(key_base, (G, NRHS)), -6.0, 6.0)
    return (base * scales * rising / 6.0).astype(jnp.float32)


def draw_halo_ids(key, part):
    owners_row = jnp.arange(N_SUB, dtype=jnp.int32)[:, None]
    left_side = jnp.arange(HB, dtype=jnp.int32)[None, :] < HB // 2
    owner = jnp.where(left_side, (owners_row - 1) % N_SUB, (owners_row + 1) % N_SUB)
    picked = jax.random.randint(jax.random.fold_in(key, 23), (N_SUB, HB), 0, GB_DEV)
    return (owner * GB_DEV + picked).astype(jnp.int32)


def touch_ends(entries, own_key, least, largest):
    longest = entries.shape.index(max(entries.shape))
    spots = []
    for shift in (0, 1):
        where = [jax.random.randint(jax.random.fold_in(own_key, axis), (), 0, length) for axis, length in enumerate(entries.shape)]
        where[longest] = (where[longest] + shift) % entries.shape[longest]
        spots.append(tuple(where))
    return entries.at[spots[0]].set(least).at[spots[1]].set(largest)


def shard_levels(stream_key, dims, cuts, low, largest):
    level = 1.0
    for position, blocks in cuts:
        draws = jax.random.uniform(jax.random.fold_in(jax.random.fold_in(stream_key, 6), position), (blocks,), jnp.float32, low / len(cuts), largest / len(cuts))
        level = level * jnp.repeat(jnp.exp(draws), dims[position] // blocks).reshape((-1,) + (1,) * (len(dims) - 1 - position))
    return level


def length_profile(number_of, total, reach, skew):
    weights = [(1 << 20) // math.isqrt(standing ** skew) + 1 for standing in range(2, number_of + 1)]
    surplus, given = total - reach - (number_of - 1), [1] * (number_of - 1)
    while surplus > 0:
        movable = [i for i in range(number_of - 1) if given[i] < reach]
        whole, left = sum([weights[i] for i in movable]), surplus
        for i in movable:
            extra = min(reach - given[i], max(1, left * weights[i] // whole), surplus)
            given[i] = given[i] + extra
            surplus = surplus - extra
    return np.array([reach] + given)


def uneven(rng, amount, total, bound, skew):
    if amount == 2:
        one = jax.random.randint(rng, (), max(1, total - bound), min(bound, total - 1) + 1)
        return jnp.stack([one, total - one])
    tallies = jnp.asarray(length_profile(amount, total, bound, skew), jnp.int32)
    twos = (amount - 1) // 2
    donor, sink = tallies[1:1 + 2 * twos:2], tallies[2:2 + 2 * twos:2]
    slack = jnp.minimum(donor - 1, bound - sink)
    shifted = jax.random.randint(jax.random.fold_in(rng, 1), (twos,), 0, 1 << 20) % (slack + 1)
    tallies = tallies.at[1:1 + 2 * twos:2].set(donor - shifted).at[2:2 + 2 * twos:2].set(sink + shifted)
    return tallies[jax.random.permutation(jax.random.fold_in(rng, 2), amount)]


def centred(key, extent, deviation, reach, cuts=(), held_as=jnp.bfloat16):
    entries = jax.random.normal(key, extent, jnp.float32) * deviation
    if len(cuts) > 0:
        entries = shard_levels(key, extent, cuts, -0.22, 0.18) * entries
    return jnp.clip(entries, min=-reach, max=reach).astype(held_as)


def setup_inputs(seed: int = 0) -> dict:
    key_of = jax.random.split(jax.random.key(seed), 9)
    return {
        "rhs": draw_rhs(jax.random.fold_in(key_of[8], 71), 0),
        "schur_diag": centred(key_of[1], (G, GB_DEV * BI), (GB_DEV * BI) ** -0.5, 0.375, ((0, 8),)),
        "precond": centred(key_of[2], (G, EXT), EXT ** -0.5, 0.25, ((0, 8),)),
        "halo_ids": draw_halo_ids(jax.random.fold_in(key_of[8], 71), 0),
        "factors": centred(key_of[4], (SLOTS, BLK, BLK), BLK ** -0.5, 0.1875, ((0, 32),)),
        "couplings": centred(key_of[5], (SLOTS, BLK, IFB * BI), (8 * IFB * BI) ** -0.5, 0.09375, ((0, 32),)),
        "block_ids": touch_ends(jax.random.randint(key_of[6], (SLOTS, IFB), 0, GBLK), jax.random.fold_in(key_of[6], 1), 0, GBLK - 1).astype(jnp.int32),
        "counts": uneven(key_of[7], DEVICES, DEVICES * NB_DEV * 5 // 8, NB_DEV, 2).astype(jnp.int32),
    }


def reference(rhs, schur_diag, precond, halo_ids, factors, couplings, block_ids, counts):
    group_rows = GB_DEV * BI
    highest = lax.Precision.HIGHEST

    def apply_schur(field):
        blocks = field.reshape(GBLK, BI, NRHS).astype(jnp.bfloat16)
        slot_index = jnp.arange(SLOTS, dtype=jnp.int32)
        live = slot_index % NB_DEV < counts[slot_index // NB_DEV]

        def step(total, item):
            factor, coupling, listed, flag = item

            def add_slot(carry):
                picked = blocks[listed].reshape(IFB * BI, NRHS)
                first = jnp.dot(coupling, picked, preferred_element_type=jnp.float32).astype(jnp.bfloat16)
                second = jnp.dot(factor, first, preferred_element_type=jnp.float32).astype(jnp.bfloat16)
                third = jnp.dot(factor.T, second, preferred_element_type=jnp.float32).astype(jnp.bfloat16)
                fourth = jnp.dot(coupling.T, third, preferred_element_type=jnp.float32)
                return carry.at[listed].add(fourth.reshape(IFB, BI, NRHS))
            return (lax.cond(flag, add_slot, lambda carry: carry, total), None)
        total, _ = lax.scan(step, jnp.zeros((GBLK, BI, NRHS), jnp.float32), (factors, couplings, block_ids, live))
        rounded = lax.optimization_barrier(field.astype(jnp.bfloat16)).astype(jnp.float32)
        local = jnp.einsum('dij,djr->dir', schur_diag.reshape(N_SUB, group_rows, group_rows).astype(jnp.float32), rounded.reshape(N_SUB, group_rows, NRHS), precision=highest)
        return 3.0 * field + local.reshape(G, NRHS) - total.reshape(G, NRHS)

    def precondition(field):
        groups = field.reshape(N_SUB, group_rows, NRHS)
        halo_rows = field.reshape(GBLK, BI, NRHS)[halo_ids].reshape(N_SUB, HB * BI, NRHS)
        extended = jnp.concatenate([groups, halo_rows], axis=1).astype(jnp.bfloat16)
        extended = lax.optimization_barrier(extended).astype(jnp.float32)
        product = jnp.einsum('dij,djr->dir', precond.reshape(N_SUB, group_rows, EXT).astype(jnp.float32), extended, precision=highest)
        return (groups + product).reshape(G, NRHS)

    def column_sums(left, right):
        return lax.optimization_barrier(jnp.sum(left * right, axis=0))
    start_norm = jnp.sqrt(column_sums(rhs, rhs))
    first_basis = rhs / start_norm
    first_dir = precondition(first_basis)
    first_image = apply_schur(first_dir)
    upper_one = column_sums(first_image, first_basis)
    rest_one = first_image - upper_one * first_basis
    length_one = jnp.sqrt(column_sums(rest_one, rest_one))
    second_basis = rest_one / length_one
    second_dir = precondition(second_basis)
    second_image = apply_schur(second_dir)
    upper_two = column_sums(second_image, first_basis)
    middle = column_sums(second_image, second_basis)
    rest_two = second_image - upper_two * first_basis - middle * second_basis
    length_two = jnp.sqrt(column_sums(rest_two, rest_two))
    radius_one = jnp.sqrt(upper_one * upper_one + length_one * length_one)
    cosine_one = upper_one / radius_one
    sine_one = length_one / radius_one
    rotated_top = cosine_one * upper_two + sine_one * middle
    rotated_low = cosine_one * middle - sine_one * upper_two
    weight_two = -rotated_low * sine_one * start_norm / (rotated_low * rotated_low + length_two * length_two)
    weight_one = (cosine_one * start_norm - rotated_top * weight_two) / radius_one
    return weight_one * first_dir + weight_two * second_dir
```

```python
import functools

import jax
import jax.numpy as jnp
from jax import lax
from jax.experimental import pallas as pl
from jax.experimental.pallas import tpu as pltpu
from jax.sharding import PartitionSpec as P

MESH = pl.DeviceIdType.MESH
F32 = jnp.float32
BF16 = jnp.bfloat16
TILE = 512


def kernel(
    n_sub,
    n_rep,
    halo_ids_hbm,
    block_ids_hbm,
    counts,
    rhs_hbm,
    schur_diag_hbm,
    precond_hbm,
    factors_hbm,
    couplings_hbm,
    out,
    halo_ids,
    block_ids,
    rhs,
    schur_diag,
    precond,
    factors,
    couplings,
    product,
    operator,
    pieces,
    halo_rhs,
    halo_w,
    dots_plane,
    dots_chain,
    field_all,
    sib_out,
    sib_in,
    mine,
    plane_out,
    plane_in,
    chain_out,
    chain_in,
    w_all,
    w_rounded,
    weight_sem,
    small_sem,
    halo_send,
    halo_recv,
    dots_send,
    dots_recv,
    chain_dots_send,
    chain_dots_recv,
    field_send,
    field_recv,
    pass_send,
    sib_send,
    sib_recv,
    plane_send,
    plane_recv,
    chain_send,
    chain_recv,
    w_send,
    w_recv,
):
    me = lax.axis_index("sub")
    layer = lax.axis_index("rep")
    core = lax.rem(me, 2)
    chip = me // 2
    sibling = me + 1 - 2 * core
    n_chip = n_sub // 2
    slots, order, width = couplings.shape
    per_slot = block_ids.shape[1]
    rows, columns = rhs.shape
    block = width // per_slot
    owned = rows // block
    share = rows // n_rep
    halo = halo_ids.shape[1]
    started = []

    def send(src, dst, send_sem, recv_sem, device):
        copy = pltpu.make_async_remote_copy(
            src_ref=src,
            dst_ref=dst,
            send_sem=send_sem,
            recv_sem=recv_sem,
            device_id=device,
            device_id_type=MESH,
        )
        copy.start()
        started.append(copy)

    def arrived(dst, send_sem, recv_sem, device):
        pltpu.make_async_remote_copy(
            src_ref=dst,
            dst_ref=dst,
            send_sem=send_sem,
            recv_sem=recv_sem,
            device_id=device,
            device_id_type=MESH,
        ).wait_recv()

    def sub_at(step):
        return lax.rem(me + step, n_sub)

    def layer_at(step):
        return lax.rem(layer + step, n_rep)

    small = [
        pltpu.make_async_copy(src, dst, small_sem.at[place])
        for place, (src, dst) in enumerate(
            (
                (rhs_hbm, rhs),
                (halo_ids_hbm, halo_ids),
                (block_ids_hbm, block_ids),
                (precond_hbm, precond),
                (schur_diag_hbm, schur_diag),
            )
        )
    ]
    for load in small:
        load.start()
    loads = []
    for slot in range(slots):
        loads.append(
            (
                pltpu.make_async_copy(
                    couplings_hbm.at[slot], couplings.at[slot], weight_sem.at[slot, 0]
                ),
                pltpu.make_async_copy(
                    factors_hbm.at[slot], factors.at[slot], weight_sem.at[slot, 1]
                ),
            )
        )
        for load in loads[slot]:
            load.start()

    barrier = pltpu.get_barrier_semaphore()
    for step in range(1, n_sub):
        pl.semaphore_signal(barrier, inc=1, device_id={"sub": sub_at(step)}, device_id_type=MESH)
    for step in range(1, n_rep):
        pl.semaphore_signal(barrier, inc=1, device_id={"rep": layer_at(step)}, device_id_type=MESH)
    pl.semaphore_wait(barrier, n_sub - 1 + n_rep - 1)

    def column_sums(left, right):
        return jnp.sum(left * right, axis=0, keepdims=True)

    def packed(sums):
        pad = jnp.zeros((8 - len(sums), columns), F32)
        return jnp.concatenate(sums + [pad], axis=0)

    def send_dots(stage, value):
        dots_plane[stage, me] = value
        for step in range(1, n_sub):
            send(
                dots_plane.at[stage, me],
                dots_plane.at[stage, me],
                dots_send.at[stage, step],
                dots_recv.at[stage, me],
                {"sub": sub_at(step)},
            )

    def total_dots(stage):
        for step in range(1, n_sub):
            source = sub_at(step)
            arrived(
                dots_plane.at[stage, source],
                dots_send.at[stage, step],
                dots_recv.at[stage, source],
                {"sub": source},
            )
        total = dots_plane[stage, 0]
        for source in range(1, n_sub):
            total = total + dots_plane[stage, source]
        return total

    def send_halo(src, dst, stage):
        send(
            src,
            dst.at[0],
            halo_send.at[stage, 0],
            halo_recv.at[stage, 0],
            {"sub": sub_at(1)},
        )
        send(
            src,
            dst.at[1],
            halo_send.at[stage, 1],
            halo_recv.at[stage, 1],
            {"sub": sub_at(n_sub - 1)},
        )

    def wait_halo(dst, stage):
        for side in range(2):
            arrived(
                dst.at[side],
                halo_send.at[stage, side],
                halo_recv.at[stage, side],
                {"sub": sub_at(n_sub - 1 if side == 0 else 1)},
            )

    def halo_rows(held):
        picked = []
        for j in range(halo):
            side = 0 if j < halo // 2 else 1
            place = lax.rem(halo_ids[0, j], owned)
            blocks = held[side].reshape(owned, block, columns).astype(F32)
            chosen = jnp.zeros((block, columns), F32)
            for b in range(owned):
                chosen = chosen + blocks[b] * jnp.where(place == b, 1.0, 0.0)
            picked.append(chosen)
        return jnp.concatenate(picked, axis=0)

    def build_operator(slot):
        for load in loads[slot]:
            load.wait()
        product[...] = jnp.zeros_like(product)

        def tile_step(tile, carry):
            start = pl.multiple_of(tile * TILE, TILE)
            image = jnp.dot(
                factors[slot, pl.ds(start, TILE), :],
                couplings[slot],
                preferred_element_type=F32,
            ).astype(BF16)
            product[...] += lax.dot_general(
                image, image, (((0,), (0,)), ((), ())), preferred_element_type=F32
            )
            return carry

        lax.fori_loop(0, order // TILE, tile_step, 0)
        leading = product[...].astype(BF16)
        operator[slot, 0] = leading
        operator[slot, 1] = (product[...] - leading.astype(F32)).astype(BF16)

    def precondition(own, halo_part):
        extended = jnp.concatenate([own.astype(BF16), halo_part.astype(BF16)], axis=0)
        return own + jnp.dot(precond[...], extended, preferred_element_type=F32)

    def own_blocks(turn):
        return field_all.at[turn, pl.ds(me * owned, owned)]

    def send_field(turn, field):
        own = own_blocks(turn)
        own[...] = field.astype(BF16).reshape(owned, block, columns)
        for step in range(1, n_chip):
            target = 2 * lax.rem(chip + step, n_chip) + core
            send(
                own,
                own,
                field_send.at[turn, step],
                field_recv.at[turn, me],
                {"sub": target},
            )
        send(
            own,
            own,
            field_send.at[turn, 0],
            field_recv.at[turn, me],
            {"sub": sibling},
        )

    def gather_field(turn):
        for step in range(1, n_chip):
            source = 2 * lax.rem(chip + step, n_chip) + core
            held = field_all.at[turn, pl.ds(source * owned, owned)]
            arrived(held, field_send.at[turn, step], field_recv.at[turn, source], {"sub": source})
            send(
                held,
                held,
                pass_send.at[turn, step],
                field_recv.at[turn, source],
                {"sub": sibling},
            )
        for step in range(n_chip):
            source = 2 * lax.rem(chip + step, n_chip) + 1 - core
            held = field_all.at[turn, pl.ds(source * owned, owned)]
            arrived(held, field_send.at[turn, 0], field_recv.at[turn, source], {"sub": sibling})

    def apply_slots(turn):
        for slot in range(slots):
            picked = jnp.concatenate(
                [field_all[turn, block_ids[slot, j]] for j in range(per_slot)], axis=0
            )
            result = jnp.dot(operator[slot, 0], picked, preferred_element_type=F32) + jnp.dot(
                operator[slot, 1], picked, preferred_element_type=F32
            )
            result = result * jnp.where(counts[0] > slot, 1.0, 0.0)
            pieces[pl.ds(slot * per_slot, per_slot)] = result.reshape(per_slot, block, columns)

    def group_sum(group):
        summed = []
        for b in range(owned):
            total = jnp.zeros((block, columns), F32)
            for slot in range(slots):
                for j in range(per_slot):
                    match = jnp.where(block_ids[slot, j] == group * owned + b, 1.0, 0.0)
                    total = total + pieces[slot * per_slot + j] * match
            summed.append(total)
        return jnp.concatenate(summed, axis=0)

    def reduce_coupled(turn):
        order_of_chips = list(range(1, n_chip)) + [0]
        for step in order_of_chips:
            target = lax.rem(chip + step, n_chip)
            sib_out[turn, step] = group_sum(2 * target + 1 - core).astype(BF16)
            send(
                sib_out.at[turn, step],
                sib_in.at[turn, step],
                sib_send.at[turn, step],
                sib_recv.at[turn, step],
                {"sub": sibling},
            )
        for step in order_of_chips:
            target = lax.rem(chip + step, n_chip)
            mine[step] = group_sum(2 * target + core)
        total = None
        for step in order_of_chips:
            arrived(
                sib_in.at[turn, step],
                sib_send.at[turn, step],
                sib_recv.at[turn, step],
                {"sub": sibling},
            )
            both = mine[step] + sib_in[turn, step].astype(F32)
            if step == 0:
                total = both
            else:
                target = 2 * lax.rem(chip + step, n_chip) + core
                plane_out[turn, step] = both.astype(BF16)
                send(
                    plane_out.at[turn, step],
                    plane_in.at[turn, step],
                    plane_send.at[turn, step],
                    plane_recv.at[turn, step],
                    {"sub": target},
                )
        for step in range(1, n_chip):
            source = 2 * lax.rem(chip + n_chip - step, n_chip) + core
            arrived(
                plane_in.at[turn, step],
                plane_send.at[turn, step],
                plane_recv.at[turn, step],
                {"sub": source},
            )
            total = total + plane_in[turn, step].astype(F32)
        chain_out[turn] = total.reshape(n_rep, share, columns)
        for step in range(1, n_rep):
            target = layer_at(step)
            send(
                chain_out.at[turn, target],
                chain_in.at[turn, step],
                chain_send.at[turn, step],
                chain_recv.at[turn, step],
                {"rep": target},
            )
        result = chain_out[turn, layer]
        for step in range(1, n_rep):
            arrived(
                chain_in.at[turn, step],
                chain_send.at[turn, step],
                chain_recv.at[turn, step],
                {"rep": layer_at(n_rep - step)},
            )
            result = result + chain_in[turn, step]
        return result

    def my_share(ref):
        return ref[pl.ds(pl.multiple_of(layer * share, share), share), :]

    def image_share(turn):
        rounded = own_blocks(turn)[...].reshape(rows, columns)
        local = jnp.dot(my_share(schur_diag), rounded, preferred_element_type=F32)
        return local - reduce_coupled(turn)

    for load in small:
        load.wait()
    send_halo(rhs, halo_rhs, 0)
    send_dots(0, packed([column_sums(rhs[...], rhs[...])]))
    build_operator(0)
    wait_halo(halo_rhs, 0)
    start_norm = jnp.sqrt(total_dots(0)[0:1])
    basis_one = rhs[...] / start_norm
    basis_one_halo = halo_rows(halo_rhs) / start_norm
    dir_one = precondition(basis_one, basis_one_halo)
    out[...] = dir_one
    send_field(0, dir_one)
    for slot in range(1, slots):
        build_operator(slot)
    gather_field(0)
    apply_slots(0)
    w_share = image_share(0) + 3.0 * my_share(out)
    w_all[layer] = w_share
    for step in range(1, n_rep):
        send(
            w_all.at[layer],
            w_all.at[layer],
            w_send.at[step],
            w_recv.at[layer],
            {"rep": layer_at(step)},
        )
    for step in range(1, n_rep):
        source = layer_at(step)
        arrived(w_all.at[source], w_send.at[step], w_recv.at[source], {"rep": source})
    image_one = w_all[...].reshape(rows, columns)
    w_rounded[...] = image_one.astype(BF16)
    send_halo(w_rounded, halo_w, 1)
    send_dots(
        1, packed([column_sums(image_one, basis_one), column_sums(image_one, image_one)])
    )
    sums = total_dots(1)
    upper_one = sums[0:1]
    length_one = jnp.sqrt(sums[1:2] - upper_one * upper_one)
    basis_two = (image_one - upper_one * basis_one) / length_one
    wait_halo(halo_w, 1)
    basis_two_halo = (halo_rows(halo_w) - upper_one * basis_one_halo) / length_one
    dir_two = precondition(basis_two, basis_two_halo)
    send_field(1, dir_two)
    mine[0] = dir_two
    dir_two_share = my_share(mine.at[0])
    mine[0] = basis_two
    basis_two_share = my_share(mine.at[0])
    basis_one_share = my_share(rhs) / start_norm
    gather_field(1)
    apply_slots(1)
    image_two = image_share(1) + 3.0 * dir_two_share
    dots_chain[layer] = packed(
        [
            column_sums(image_two, basis_one_share),
            column_sums(image_two, basis_two_share),
            column_sums(image_two, image_two),
        ]
    )
    for step in range(1, n_rep):
        send(
            dots_chain.at[layer],
            dots_chain.at[layer],
            chain_dots_send.at[step],
            chain_dots_recv.at[layer],
            {"rep": layer_at(step)},
        )
    for step in range(1, n_rep):
        source = layer_at(step)
        arrived(
            dots_chain.at[source],
            chain_dots_send.at[step],
            chain_dots_recv.at[source],
            {"rep": source},
        )
    chain_total = dots_chain[0]
    for source in range(1, n_rep):
        chain_total = chain_total + dots_chain[source]
    send_dots(2, chain_total)
    sums = total_dots(2)
    upper_two = sums[0:1]
    middle = sums[1:2]
    length_two_squared = sums[2:3] - upper_two * upper_two - middle * middle
    radius_one = jnp.sqrt(upper_one * upper_one + length_one * length_one)
    cosine_one = upper_one / radius_one
    sine_one = length_one / radius_one
    rotated_top = cosine_one * upper_two + sine_one * middle
    rotated_low = cosine_one * middle - sine_one * upper_two
    weight_two = (
        -rotated_low * sine_one * start_norm / (rotated_low * rotated_low + length_two_squared)
    )
    weight_one = (cosine_one * start_norm - rotated_top * weight_two) / radius_one
    out[...] = weight_one * out[...] + weight_two * dir_two
    for copy in started:
        copy.wait_send()


def on_device(rhs, schur_diag, precond, halo_ids, factors, couplings, block_ids, counts):
    n_sub = lax.axis_size("sub")
    n_rep = lax.axis_size("rep")
    n_chip = n_sub // 2
    rows, columns = rhs.shape
    slots, order, width = couplings.shape
    per_slot = block_ids.shape[1]
    block = width // per_slot
    owned = rows // block
    share = rows // n_rep
    dma = pltpu.SemaphoreType.DMA
    hbm = pl.BlockSpec(memory_space=pltpu.HBM)
    return pl.pallas_call(
        functools.partial(kernel, n_sub, n_rep),
        out_shape=jax.ShapeDtypeStruct((rows, columns), F32),
        in_specs=[hbm, hbm, pl.BlockSpec(memory_space=pltpu.SMEM)] + [hbm] * 5,
        out_specs=pl.BlockSpec(memory_space=pltpu.VMEM),
        scratch_shapes=[
            pltpu.SMEM(halo_ids.shape, jnp.int32),
            pltpu.SMEM(block_ids.shape, jnp.int32),
            pltpu.VMEM(rhs.shape, F32),
            pltpu.VMEM(schur_diag.shape, BF16),
            pltpu.VMEM(precond.shape, BF16),
            pltpu.VMEM(factors.shape, BF16),
            pltpu.VMEM(couplings.shape, BF16),
            pltpu.VMEM((width, width), F32),
            pltpu.VMEM((slots, 2, width, width), BF16),
            pltpu.VMEM((slots * per_slot, block, columns), F32),
            pltpu.VMEM((2, rows, columns), F32),
            pltpu.VMEM((2, rows, columns), BF16),
            pltpu.VMEM((3, n_sub, 8, columns), F32),
            pltpu.VMEM((n_rep, 8, columns), F32),
            pltpu.VMEM((2, n_sub * owned, block, columns), BF16),
            pltpu.VMEM((2, n_chip, rows, columns), BF16),
            pltpu.VMEM((2, n_chip, rows, columns), BF16),
            pltpu.VMEM((n_chip, rows, columns), F32),
            pltpu.VMEM((2, n_chip, rows, columns), BF16),
            pltpu.VMEM((2, n_chip, rows, columns), BF16),
            pltpu.VMEM((2, n_rep, share, columns), F32),
            pltpu.VMEM((2, n_rep, share, columns), F32),
            pltpu.VMEM((n_rep, share, columns), F32),
            pltpu.VMEM((rows, columns), BF16),
            dma((slots, 2)),
            dma((5,)),
            dma((2, 2)),
            dma((2, 2)),
            dma((3, n_sub)),
            dma((3, n_sub)),
            dma((n_rep,)),
            dma((n_rep,)),
            dma((2, n_chip)),
            dma((2, n_sub)),
            dma((2, n_chip)),
            dma((2, n_chip)),
            dma((2, n_chip)),
            dma((2, n_chip)),
            dma((2, n_chip)),
            dma((2, n_rep)),
            dma((2, n_rep)),
            dma((n_rep,)),
            dma((n_rep,)),
        ],
        compiler_params=pltpu.CompilerParams(
            collective_id=0, has_side_effects=True, vmem_limit_bytes=63 * 1024 * 1024
        ),
        cost_estimate=pl.CostEstimate(
            flops=slots * 2 * order * width * (order + width),
            bytes_accessed=slots * 2 * order * (order + width),
            transcendentals=0,
        ),
    )(halo_ids, block_ids, counts, rhs, schur_diag, precond, factors, couplings)


def solution(mesh):
    placed = (
        P("sub", None),
        P("sub", None),
        P("sub", None),
        P("sub", None),
        P(("sub", "rep"), None, None),
        P(("sub", "rep"), None, None),
        P(("sub", "rep"), None),
        P(("sub", "rep")),
    )
    return jax.shard_map(
        on_device, mesh=mesh, in_specs=placed, out_specs=P("sub", None), check_vma=False
    )
```
